128 devices in a mesh: col: 8 (over z, core), row: 16 (over x, y).
Axes of the slice: x: 4, y: 4, z: 4, core: 2. Of those that a mesh axis runs over, the one named last changes fastest.
Arguments:
- affinity: bfloat16 [15360, 128, 128], P(('col', 'row')), may hold values from 0 to 0.015625
- tile_rows: int32 [15360], P(('col', 'row')), may hold values from 0 to 39
- tile_cols: int32 [15360], P(('col', 'row')), may hold values from 0 to 79
- live_tiles: int32 [128], P(('col', 'row')), may hold values from 1 to 120, as said below
- start: float32 [81920, 256], P(('col', 'row')), may hold values from -1500 to 1500
Outputs:
- vectors: float32 [81920, 256], P(('col', 'row'))
- first_passes: float32 [2, 81920, 256], P(None, ('col', 'row'))
The draws below stay inside these ranges and needn't reach their ends.
Inputs may be any that keep to these rules, and one draw needn't show every extreme that they name: A device's tiles are its slots 0 to live_tiles - 1; later slots are ignored. Some device holds exactly 120 tiles.
All inputs are finite; a program needn't handle non-finite values.
Results may differ from the reference program's by a relative error of at most 0.0003.
Values sent between devices are 32-bit elements; how exact they have to be, the bound alone decides.
A program may use at most 128 MiB of HBM per device.

```python
import math
import jax
import jax.numpy as jnp
from jax import lax

TILE = 128
VECS = 256
ITERS = 2
TROWS_DEV = 5
NIMG = 81920
SLOTS = 120
ROWSET_T = 40
COLBLK_T = 80
N_ROW = 16
DEVICES = 128


def draw_live_tiles(key, part):
    first_key, second_key, third_key = jax.random.split(key, 3)
    draws_one = jax.random.randint(first_key, (DEVICES,), 1, SLOTS + 1)
    draws_two = jax.random.randint(second_key, (DEVICES,), 1, SLOTS + 1)
    counts = jnp.minimum(draws_one, draws_two)
    busiest = jax.random.randint(third_key, (), 0, DEVICES)
    counts = jnp.where(jnp.arange(DEVICES) == busiest, SLOTS, counts)
    return counts.astype(jnp.int32)


def draw_start(key, part):
    base_key, rows_key, cols_key = jax.random.split(jax.random.fold_in(key, 7), 3)
    base = jnp.clip(jax.random.normal(base_key, (NIMG, VECS), jnp.float32), -5.0, 5.0)
    row_scale = jnp.exp(jax.random.uniform(rows_key, (NIMG, 1), jnp.float32, 0.0, math.log(10.0)))
    rising = jnp.exp(math.log(3.0) * jnp.arange(NIMG, dtype=jnp.float32) / NIMG)[:, None]
    col_scale = jnp.exp(jax.random.uniform(cols_key, (1, VECS), jnp.float32, 0.0, math.log(10.0)))
    return (base * row_scale * rising * col_scale).astype(jnp.float32)


def plant(drawn, own_key, smallest, largest):
    extent = drawn.shape
    index_at = [jax.random.randint(jax.random.fold_in(own_key, axis), (), 0, extent[axis]) for axis in range(len(extent))]
    drawn = drawn.at[tuple(index_at)].set(smallest)
    longest = extent.index(max(extent))
    index_at[longest] = (index_at[longest] + 1) % extent[longest]
    return drawn.at[tuple(index_at)].set(largest)


def levels(stream_key, extent, pieces, low, top_value):
    level, own = 1.0, jax.random.fold_in(stream_key, 6)
    for dim, parts in pieces:
        draws = jnp.exp(jax.random.uniform(jax.random.fold_in(own, dim), (parts,), jnp.float32, low / len(pieces), top_value / len(pieces)))
        level = level * jnp.repeat(draws, extent[dim] // parts).reshape([-1 if axis == dim else 1 for axis in range(len(extent))])
    return level


def setup_inputs(seed: int = 0) -> dict:
    key_list = jax.random.split(jax.random.key(seed), 6)
    affinity = jnp.clip(0.015625 * jax.random.uniform(key_list[0], (DEVICES * SLOTS, TILE, TILE), jnp.float32) ** levels(key_list[0], (DEVICES * SLOTS, TILE, TILE), ((0, 128),), -0.2, 0.2), 0.0, 0.015625).astype(jnp.bfloat16)
    tile_rows = plant(jax.random.randint(key_list[1], (DEVICES * SLOTS,), 0, ROWSET_T), jax.random.fold_in(key_list[1], 1), 0, ROWSET_T - 1).astype(jnp.int32)
    tile_cols = plant(jax.random.randint(key_list[2], (DEVICES * SLOTS,), 0, COLBLK_T), jax.random.fold_in(key_list[2], 1), 0, COLBLK_T - 1).astype(jnp.int32)
    live_tiles = draw_live_tiles(jax.random.fold_in(key_list[5], 71), 0)
    start = draw_start(jax.random.fold_in(key_list[5], 71), 0)
    return dict(affinity=affinity, tile_rows=tile_rows, tile_cols=tile_cols, live_tiles=live_tiles, start=start)


highest = lax.Precision.HIGHEST

def inverse_factor(matrix):
    gram = jnp.dot(matrix.T.astype(jnp.float32), matrix.astype(jnp.float32), precision=highest, preferred_element_type=jnp.float32)
    lower = jnp.linalg.cholesky(gram)
    return jax.scipy.linalg.solve_triangular(lower, jnp.eye(VECS, dtype=jnp.float32), lower=True)

def normalize(matrix):
    return jnp.dot(matrix.astype(jnp.float32), inverse_factor(matrix).T.astype(jnp.float32), precision=highest, preferred_element_type=jnp.float32)

def accumulate(affinity, tile_rows, tile_cols, live_tiles, initial, contribution):

    def device_step(device, totals):
        dev_col = device // N_ROW
        dev_row = device % N_ROW

        def slot_step(slot_number, partial_acc):
            flat_index = device * SLOTS + slot_number
            tile_row = tile_rows[flat_index]
            target = (tile_row // TROWS_DEV * N_ROW + dev_row) * TROWS_DEV + tile_row % TROWS_DEV
            source = dev_col * N_ROW * TROWS_DEV + tile_cols[flat_index]
            square = lax.dynamic_index_in_dim(affinity, flat_index, 0, keepdims=False).astype(jnp.float32)
            current = lax.dynamic_index_in_dim(partial_acc, target, 0, keepdims=False)
            return lax.dynamic_update_index_in_dim(partial_acc, current + contribution(square, source), target, 0)
        return lax.fori_loop(jnp.int32(0), live_tiles[device], slot_step, totals)
    return lax.fori_loop(jnp.int32(0), jnp.int32(DEVICES), device_step, initial)

def row_total(square, source):
    return lax.optimization_barrier(jnp.sum(square, axis=1))

def reference(affinity, tile_rows, tile_cols, live_tiles, start):
    totals = accumulate(affinity, tile_rows, tile_cols, live_tiles, jnp.zeros((NIMG // TILE, TILE), jnp.float32), row_total)
    degree = 1.0 + totals.reshape(NIMG)
    scaling = (1.0 / jnp.sqrt(degree))[:, None]
    basis = start
    firsts = []
    for step_number in range(ITERS):
        scaled = scaling * basis
        tiled_panels = scaled.reshape(NIMG // TILE, TILE, VECS)

        def product(square, source):
            panel_rows = lax.dynamic_index_in_dim(tiled_panels, source, 0, keepdims=False)
            return jnp.dot(square.astype(jnp.float32), panel_rows.astype(jnp.float32), precision=highest, preferred_element_type=jnp.float32)
        image = accumulate(affinity, tile_rows, tile_cols, live_tiles, jnp.zeros((NIMG // TILE, TILE, VECS), jnp.float32), product)
        image_block = scaling * (scaled + image.reshape(NIMG, VECS))
        first = normalize(image_block)
        firsts.append(first)
        basis = normalize(first)
    root = jnp.sqrt(jnp.float32(NIMG))
    return (root * basis, root * jnp.stack(firsts, axis=0))
```

```python
import functools

import jax
import jax.numpy as jnp
from jax import lax
from jax.experimental import pallas as pl
from jax.experimental.pallas import tpu as pltpu
from jax.sharding import Mesh
from jax.sharding import PartitionSpec as P

Z, K, X, Y = "z", "k", "x", "y"
COL_ROW = (Z, K, X, Y)
ITERS = 2
TILE = 128
VECS = 256
OWN = 5
ROWS = OWN * TILE
GROUPS = 16
DESTS = 8
SLOTS = 120
HALF = 128
ROUTE = ROWS // 2
SUB = ROUTE // 2
BLOCK = 32
HIGHEST = lax.Precision.HIGHEST
MESH = pl.DeviceIdType.MESH
F32 = jnp.float32


def matmul(a, b, contract=((1,), (0,))):
    return lax.dot_general(
        a, b, (contract, ((), ())), precision=HIGHEST, preferred_element_type=F32
    )


def block_inverse(block):
    rows = lax.broadcasted_iota(jnp.int32, (BLOCK, 128), 0)
    lanes = lax.broadcasted_iota(jnp.int32, (BLOCK, 128), 1)
    e = jnp.where(lanes < BLOCK, block, jnp.where(lanes - BLOCK == rows, 1.0, 0.0))
    pivots = jnp.ones((BLOCK, 128), F32)
    for panel in range(BLOCK // 8):
        cols = [
            jnp.broadcast_to(e[:, 8 * panel + j : 8 * panel + j + 1], (BLOCK, 128))
            for j in range(8)
        ]
        for j in range(8):
            k = 8 * panel + j
            d = cols[j][k : k + 1, :]
            pivots = jnp.where(rows == k, d, pivots)
            f = jnp.where(rows > k, cols[j] * (1.0 / d), 0.0)
            for i in range(j + 1, 8):
                cols[i] = cols[i] - f * cols[i][k : k + 1, :]
            e = e - f * e[k : k + 1, :]
    return e * lax.rsqrt(pivots)


def inverse_factor(gram, aug):
    aug[:, 0:VECS] = gram
    r = lax.broadcasted_iota(jnp.int32, (VECS, VECS), 0)
    c = lax.broadcasted_iota(jnp.int32, (VECS, VECS), 1)
    aug[:, VECS:] = jnp.where(r == c, 1.0, 0.0)
    for k0 in range(0, VECS, BLOCK):
        lo = k0 // 128 * 128
        hi = VECS + (k0 + BLOCK + 127) // 128 * 128
        block = aug[k0 : k0 + BLOCK, lo : lo + 128]
        if k0 > lo:
            block = pltpu.roll(block, 128 - (k0 - lo), 1)
        inverse = block_inverse(block)[:, BLOCK : 2 * BLOCK]
        panel = matmul(inverse, aug[k0 : k0 + BLOCK, lo:hi])
        aug[k0 : k0 + BLOCK, lo:hi] = panel
        if k0 + BLOCK < VECS:
            below = panel[:, : VECS - lo].T[k0 + BLOCK - lo :, :]
            aug[k0 + BLOCK :, lo:hi] = aug[k0 + BLOCK :, lo:hi] - matmul(below, panel)
    return aug[:, VECS:]


def place(axis, offset):
    return lax.rem(lax.axis_index(axis) + (offset + 4), 4)


class Sems:
    def __init__(self, send, recv):
        self.send, self.recv, self.used = send, recv, 0

    def copy(self, src, dst, device):
        i = self.used
        self.used += 1
        return pltpu.make_async_remote_copy(
            src_ref=src,
            dst_ref=dst,
            send_sem=self.send.at[i],
            recv_sem=self.recv.at[i],
            device_id=device,
            device_id_type=MESH,
        )


class Gather:
    def __init__(self, field, sems):
        self.field, self.sems, self.all = field, sems, []
        self.p1, self.q, self.f1, self.f2 = {}, {}, {}, {}

    def slot(self, route, d1, d2):
        dx, dy = (d1, d2) if route == 0 else (d2, d1)
        return place(X, dx) * 4 + place(Y, dy)

    def send(self, route, slot, start, size, along, sign):
        axis = (X, Y)[route ^ along]
        part = self.field.at[slot, pl.ds(route * ROUTE + start, size)]
        c = self.sems.copy(part, part, {axis: place(axis, sign)})
        c.start()
        self.all.append(c)
        return c

    def begin(self):
        for route in (0, 1):
            for s in (1, -1):
                self.p1[route, s] = self.send(route, self.slot(route, 0, 0), 0, ROUTE, 0, s)
        for route in (0, 1):
            self.spread(route, 0)

    def spread(self, route, d1):
        for s in (1, -1):
            self.q[route, d1, s] = self.send(route, self.slot(route, d1, 0), 0, ROUTE, 1, s)

    def sub(self, sign):
        return 0 if sign > 0 else SUB

    def near(self):
        for route in (0, 1):
            for s in (1, -1):
                self.p1[route, s].wait_recv()
                self.f1[route, s] = self.send(
                    route, self.slot(route, -s, 0), self.sub(s), SUB, 0, s
                )
        for route in (0, 1):
            for s in (1, -1):
                self.spread(route, -s)

    def far(self):
        for route in (0, 1):
            for s in (1, -1):
                self.f1[route, s].wait_recv()
            self.spread(route, 2)

    def onward(self, which):
        for d1 in which:
            for route in (0, 1):
                for s in (1, -1):
                    self.q[route, d1, s].wait_recv()
                    self.f2[route, d1, s] = self.send(
                        route, self.slot(route, d1, -s), self.sub(s), SUB, 1, s
                    )

    def finish(self):
        for c in self.f2.values():
            c.wait_recv()

    def sent(self):
        for c in self.all:
            c.wait_send()


class Scatter:
    def __init__(self, terms, pair, arrived, sems):
        self.terms, self.pair, self.arrived, self.sems = terms, pair, arrived, sems
        self.all, self.first, self.direct, self.last = [], {}, {}, {}

    def go(self, src, dst, device):
        c = self.sems.copy(src, dst, device)
        c.start()
        self.all.append(c)
        return c

    def begin(self):
        other = 1 - lax.axis_index(K)
        for d in (2, 1, -1, 0):
            self.first[d] = self.go(
                self.terms.at[other, place(Z, d)], self.pair.at[d % 4], {K: other}
            )

    def combine(self, d):
        self.first[d].wait_recv()
        mine = lax.axis_index(K)
        self.pair[d % 4] = self.pair[d % 4] + self.terms[mine, place(Z, d)]

    def rows(self, part):
        return pl.ds(part * ROUTE, ROUTE)

    def ring(self):
        self.combine(2)
        for part, s in ((0, 1), (1, -1)):
            self.direct[2, s] = self.go(
                self.pair.at[2, self.rows(part)], self.arrived.at[part], {Z: place(Z, s)}
            )
        for part, s in ((1, 1), (0, -1)):
            self.combine(s)
            self.direct[1, s] = self.go(
                self.pair.at[s % 4, self.rows(part)], self.arrived.at[2 + part], {Z: place(Z, s)}
            )
        for part, s in ((0, 1), (1, -1)):
            self.direct[2, s].wait_recv()
            self.pair[s % 4, self.rows(part)] = (
                self.pair[s % 4, self.rows(part)] + self.arrived[part]
            )
            self.last[s] = self.go(
                self.pair.at[s % 4, self.rows(part)], self.arrived.at[4 + part], {Z: place(Z, s)}
            )
        self.combine(0)

    def total(self, put):
        for s in (1, -1):
            self.direct[1, s].wait_recv()
            self.last[s].wait_recv()
        for part in (0, 1):
            put(
                part,
                self.pair[0, self.rows(part)] + self.arrived[2 + part] + self.arrived[4 + part],
            )

    def sent(self):
        for c in self.all:
            c.wait_send()


class GramSum:
    def __init__(self, own, parts, piece, pieces, whole, sems):
        self.own, self.parts, self.piece, self.pieces, self.whole = own, parts, piece, pieces, whole
        self.sems, self.all = sems, []

    def go(self, src, dst, device):
        c = self.sems.copy(src, dst, device)
        c.start()
        self.all.append(c)
        return c

    def peers(self):
        for dx in range(4):
            for dy in range(4):
                if dx or dy:
                    yield place(X, dx), place(Y, dy)

    def begin(self):
        me = lax.axis_index(X) * 4 + lax.axis_index(Y)
        self.one = [
            self.go(self.own.at[x * 4 + y], self.parts.at[me], {X: x, Y: y})
            for x, y in self.peers()
        ]
        self.parts[me] = self.own[me]

    def across(self):
        for c in self.one:
            c.wait_recv()
        total = self.parts[0]
        for i in range(1, GROUPS):
            total = total + self.parts[i]
        self.piece[...] = total
        z, k = lax.axis_index(Z), lax.axis_index(K)
        me = z * 2 + k
        self.two = []
        for dk in range(2):
            for dz in range(4):
                if dk or dz:
                    to = {Z: place(Z, dz), K: lax.rem(k + dk, 2)}
                    self.two.append(self.go(self.piece, self.pieces.at[me], to))
        self.pieces[me] = total

    def back(self):
        for c in self.two:
            c.wait_recv()
        total = self.pieces[0]
        for i in range(1, DESTS):
            total = total + self.pieces[i]
        me = lax.axis_index(X) * 4 + lax.axis_index(Y)
        self.whole[me] = total
        self.three = [
            self.go(self.whole.at[me], self.whole.at[me], {X: x, Y: y}) for x, y in self.peers()
        ]

    def result(self):
        for c in self.three:
            c.wait_recv()
        return self.whole[...].reshape(VECS, VECS)

    def sent(self):
        for c in self.all:
            c.wait_send()


GRAM_COPIES = 15 + 7 + 15
GATHER_COPIES = 40
SCATTER_COPIES = 10


def gram_scratch():
    return [
        pltpu.VMEM((GROUPS, 16, VECS), F32),
        pltpu.VMEM((GROUPS, 16, VECS), F32),
        pltpu.VMEM((16, VECS), F32),
        pltpu.VMEM((DESTS, 16, VECS), F32),
        pltpu.VMEM((GROUPS, 16, VECS), F32),
        pltpu.SemaphoreType.DMA((GRAM_COPIES,)),
        pltpu.SemaphoreType.DMA((GRAM_COPIES,)),
    ]


def gram_of(refs):
    return GramSum(*refs[:5], Sems(*refs[5:]))


def split_panels(field, split, scale):
    def group(r, _):
        if scale is not None:
            cols = scale[r].T
        for t in range(OWN):
            v = field[r, pl.ds(t * TILE, TILE), :]
            if scale is not None:
                v = v * cols[:, t : t + 1]
            high = v.astype(jnp.bfloat16)
            split[r * OWN + t, 0:TILE, :] = high
            split[r * OWN + t, TILE:, :] = (v - high.astype(F32)).astype(jnp.bfloat16)
        return 0

    lax.fori_loop(0, GROUPS, group, 0)


UNROLL = 8


def tile_products(tiles, split, order, source, keep, running):
    def step(i, total):
        for j in range(UNROLL):
            s = i * UNROLL + j
            tile = tiles[order[s]]
            both = jnp.concatenate([tile, tile], axis=1)
            y = jnp.dot(both, split[source[s]], preferred_element_type=F32)
            total = y + keep[s] * total
            running[s] = total
        return total

    lax.fori_loop(0, SLOTS // UNROLL, step, jnp.zeros((TILE, HALF), F32))


def tile_terms(running, last, has, terms):
    def dest(c, _):
        z, k = c // 2, lax.rem(c, 2)
        for t in range(OWN):
            i = c * OWN + t
            terms[k, z, pl.ds(t * TILE, TILE), :] = has[i] * running[last[i]]
        return 0

    lax.fori_loop(0, DESTS, dest, 0)


def load_tiles(affinity, tiles, sem):
    c = pltpu.make_async_copy(affinity, tiles, sem)
    c.start()
    return c


def spread_scale(row, scale):
    cols = row[...].T
    for t in range(OWN):
        scale[pl.ds(t * TILE, TILE), :] = jnp.broadcast_to(cols[:, t : t + 1], (TILE, 128))


def half(h):
    return pl.ds(h * HALF, HALF)


def first_kernel(
    order, source, keep, last, has, start, affinity, image, scale,
    tiles, field, split, running, terms, pair, arrived, sums, degree_out, degree_in, scales,
    tile_sem, gather_send, gather_recv, scatter_send, scatter_recv, small_send, small_recv,
):
    tile_copy = load_tiles(affinity, tiles, tile_sem)
    x, y, z, k = (lax.axis_index(a) for a in (X, Y, Z, K))
    me, col = x * 4 + y, z * 2 + k
    gathers = [
        Gather(field.at[h], Sems(gather_send.at[h], gather_recv.at[h])) for h in range(2)
    ]
    scatters = [
        Scatter(terms.at[h], pair.at[h], arrived.at[h], Sems(scatter_send.at[h], scatter_recv.at[h]))
        for h in range(2)
    ]
    small = Sems(small_send, small_recv)
    smalls = []
    for h in range(2):
        field[h, me] = start[:, h * HALF : (h + 1) * HALF]
    gathers[0].begin()
    tile_copy.wait()

    ones = jnp.ones((8, TILE), jnp.bfloat16)

    def row_sums(i, total):
        for j in range(UNROLL):
            s = i * UNROLL + j
            d = lax.dot_general(
                ones, tiles[order[s]], (((1,), (1,)), ((), ())), preferred_element_type=F32
            )
            total = d + keep[s] * total
            sums[s] = total
        return total

    lax.fori_loop(0, SLOTS // UNROLL, row_sums, jnp.zeros((8, TILE), F32))
    for c in range(DESTS):
        for t in range(8):
            i = c * OWN + t
            if t < OWN:
                degree_out[c, t : t + 1, :] = (has[i] * sums[last[i]])[0:1]
            else:
                degree_out[c, t : t + 1, :] = jnp.zeros((1, TILE), F32)
    for dk in range(2):
        for dz in range(4):
            if dk or dz:
                pz, pk = place(Z, dz), lax.rem(k + dk, 2)
                c = small.copy(degree_out.at[pz * 2 + pk], degree_in.at[col], {Z: pz, K: pk})
                c.start()
                smalls.append(c)
    degree_in[col] = degree_out[col]
    gathers[0].near()
    for c in smalls:
        c.wait_recv()
    degree = degree_in[0]
    for c in range(1, DESTS):
        degree = degree + degree_in[c]
    scales[me] = 1.0 / jnp.sqrt(1.0 + degree)
    gathered = []
    for dx in range(4):
        for dy in range(4):
            if dx or dy:
                c = small.copy(
                    scales.at[me], scales.at[me], {X: place(X, dx), Y: place(Y, dy)}
                )
                c.start()
                gathered.append(c)
    spread_scale(scales.at[me], scale)
    gathers[0].far()
    gathers[1].begin()
    gathers[0].onward((0, 1, -1, 2))
    for c in gathered:
        c.wait_recv()
    gathers[1].near()
    gathers[0].finish()

    def products(h):
        split_panels(field.at[h], split, scales)
        tile_products(tiles, split, order, source, keep, running)
        tile_terms(running, last, has, terms.at[h])
        scatters[h].begin()

    products(0)
    gathers[1].far()
    scatters[0].ring()
    gathers[1].onward((0, 1, -1, 2))
    gathers[1].finish()
    products(1)
    scatters[1].ring()

    def put(h, part, total):
        rows = pl.ds(part * ROUTE, ROUTE)
        s = scale[rows]
        image[rows, half(h)] = s * (s * start[rows, half(h)] + total)

    for h in range(2):
        scatters[h].total(functools.partial(put, h))
    for c in smalls + gathered:
        c.wait_send()
    for h in range(2):
        gathers[h].sent()
        scatters[h].sent()


def second_kernel(
    order, source, keep, last, has, image, scale, affinity, vectors, firsts,
    tiles, field, split, running, terms, pair, arrived, aug, work,
    tile_sem, gather_send, gather_recv, scatter_send, scatter_recv, *gram_refs,
):
    tile_copy = load_tiles(affinity, tiles, tile_sem)
    x, y = (lax.axis_index(a) for a in (X, Y))
    me = x * 4 + y
    gathers = [
        Gather(field.at[h], Sems(gather_send.at[h], gather_recv.at[h])) for h in range(2)
    ]
    scatters = [
        Scatter(terms.at[h], pair.at[h], arrived.at[h], Sems(scatter_send.at[h], scatter_recv.at[h]))
        for h in range(2)
    ]
    grams = [gram_of(gram_refs[7 * i : 7 * i + 7]) for i in range(4)]
    root = jnp.sqrt(F32(ROWS * GROUPS * DESTS))

    def local_gram(g, matrix):
        grams[g].own[...] = matmul(matrix, matrix, ((0,), (0,))).reshape(GROUPS, 16, VECS)
        grams[g].begin()

    for h in range(2):
        field[h, me] = scale[...] * image[:, half(h)]
    gathers[0].begin()
    local_gram(0, image[...])
    gathers[0].near()
    grams[0].across()
    gathers[0].far()
    gathers[1].begin()
    grams[0].back()
    inverse_one = inverse_factor(grams[0].result(), aug)
    gathers[0].onward((0, 1, -1, 2))
    first = matmul(image[...], inverse_one, ((1,), (1,)))
    firsts[0] = root * first
    work[0] = inverse_one
    local_gram(1, first)
    gathers[1].near()
    grams[1].across()
    tile_copy.wait()

    def products(h):
        split_panels(field.at[h], split, None)
        tile_products(tiles, split, order, source, keep, running)
        tile_terms(running, last, has, terms.at[h])
        scatters[h].begin()

    gathers[0].finish()
    gathers[1].far()
    grams[1].back()
    products(0)
    gathers[1].onward((0, 1, -1, 2))
    scatters[0].ring()
    gathers[1].finish()
    products(1)
    scatters[1].ring()
    inverse_two = inverse_factor(grams[1].result(), aug)
    both = matmul(inverse_two, work[0])

    def put(h, part, total):
        rows = pl.ds(part * ROUTE, ROUTE)
        s = scale[rows]
        vectors[rows, half(h)] = s * (s * image[rows, half(h)] + total)

    for h in range(2):
        scatters[h].total(functools.partial(put, h))
    mapped = matmul(vectors[...], both, ((1,), (1,)))
    local_gram(2, mapped)
    grams[2].across()
    grams[2].back()
    first = matmul(mapped, inverse_factor(grams[2].result(), aug), ((1,), (1,)))
    local_gram(3, first)
    firsts[1] = root * first
    grams[3].across()
    grams[3].back()
    vectors[...] = root * matmul(first, inverse_factor(grams[3].result(), aug), ((1,), (1,)))
    for h in range(2):
        gathers[h].sent()
        scatters[h].sent()
    for g in grams:
        g.sent()


def sweep_scratch():
    return [
        pltpu.VMEM((SLOTS, TILE, TILE), jnp.bfloat16),
        pltpu.VMEM((2, GROUPS, ROWS, HALF), F32),
        pltpu.VMEM((GROUPS * OWN, 2 * TILE, HALF), jnp.bfloat16),
        pltpu.VMEM((SLOTS, TILE, HALF), F32),
        pltpu.VMEM((2, 2, 4, ROWS, HALF), F32),
        pltpu.VMEM((2, 4, ROWS, HALF), F32),
        pltpu.VMEM((2, 6, ROUTE, HALF), F32),
    ]


def sweep_semaphores():
    return [
        pltpu.SemaphoreType.DMA,
        pltpu.SemaphoreType.DMA((2, GATHER_COPIES)),
        pltpu.SemaphoreType.DMA((2, GATHER_COPIES)),
        pltpu.SemaphoreType.DMA((2, SCATTER_COPIES)),
        pltpu.SemaphoreType.DMA((2, SCATTER_COPIES)),
    ]


def slot_order(tile_rows, tile_cols, live_tiles):
    slot = jnp.arange(SLOTS)
    key = jnp.where(slot < live_tiles[0], tile_rows, DESTS * OWN)
    before = (key[None, :] < key[:, None]) | (
        (key[None, :] == key[:, None]) & (slot[None, :] < slot[:, None])
    )
    rank = jnp.sum(before.astype(jnp.int32), axis=1)
    at = rank[None, :] == slot[:, None]
    order = jnp.sum(jnp.where(at, slot[None, :], 0), axis=1)
    source = jnp.sum(jnp.where(at, tile_cols[None, :], 0), axis=1)
    follows = (rank[None, :] == slot[:, None] - 1).astype(jnp.int32)
    keys = jnp.sum(jnp.where(at, key[None, :], 0), axis=1)
    previous = jnp.sum(follows * (key[None, :] + 1), axis=1) - 1
    keep = (keys == previous).astype(F32)
    row = jnp.arange(DESTS * OWN)
    last = jnp.maximum(jnp.sum((key[None, :] <= row[:, None]).astype(jnp.int32), axis=1) - 1, 0)
    has = jnp.any(key[None, :] == row[:, None], axis=1).astype(F32)
    return order.astype(jnp.int32), source.astype(jnp.int32), keep, last, has


def body(affinity, tile_rows, tile_cols, live_tiles, start):
    slots = slot_order(tile_rows, tile_cols, live_tiles)
    smem = pl.BlockSpec(memory_space=pltpu.SMEM)
    vmem = pl.BlockSpec(memory_space=pltpu.VMEM)
    anywhere = pl.BlockSpec(memory_space=pl.ANY)
    params = pltpu.CompilerParams(has_side_effects=True, vmem_limit_bytes=56 << 20)
    image, scale = pl.pallas_call(
        first_kernel,
        out_shape=(
            jax.ShapeDtypeStruct((ROWS, VECS), F32),
            jax.ShapeDtypeStruct((ROWS, HALF), F32),
        ),
        in_specs=[smem] * 5 + [vmem, anywhere],
        out_specs=(vmem, vmem),
        scratch_shapes=sweep_scratch()
        + [
            pltpu.VMEM((SLOTS, 8, TILE), F32),
            pltpu.VMEM((DESTS, 8, TILE), F32),
            pltpu.VMEM((DESTS, 8, TILE), F32),
            pltpu.VMEM((GROUPS, 8, TILE), F32),
        ]
        + sweep_semaphores()
        + [pltpu.SemaphoreType.DMA((22,)), pltpu.SemaphoreType.DMA((22,))],
        compiler_params=params,
        name="first_sweep",
    )(*slots, start, affinity)
    vectors, firsts = pl.pallas_call(
        second_kernel,
        out_shape=(
            jax.ShapeDtypeStruct((ROWS, VECS), F32),
            jax.ShapeDtypeStruct((ITERS, ROWS, VECS), F32),
        ),
        in_specs=[smem] * 5 + [vmem, vmem, anywhere],
        out_specs=(vmem, vmem),
        scratch_shapes=sweep_scratch()
        + [pltpu.VMEM((VECS, 2 * VECS), F32), pltpu.VMEM((1, VECS, VECS), F32)]
        + sweep_semaphores()
        + gram_scratch() * 4,
        compiler_params=params,
        name="second_sweep",
    )(*slots, image, scale, affinity)
    return vectors, firsts


def solution(mesh):
    torus = Mesh(mesh.devices.reshape(4, 2, 4, 4), COL_ROW)
    return jax.shard_map(
        body,
        mesh=torus,
        in_specs=(P(COL_ROW, None, None), P(COL_ROW), P(COL_ROW), P(COL_ROW), P(COL_ROW, None)),
        out_specs=(P(COL_ROW, None), P(None, COL_ROW, None)),
        check_vma=False,
    )
```

```python
import functools

import jax
import jax.numpy as jnp
from jax import lax
from jax.experimental import pallas as pl
from jax.experimental.pallas import tpu as pltpu
from jax.sharding import Mesh
from jax.sharding import PartitionSpec as P

Z, K, X, Y = "z", "k", "x", "y"
COL_ROW = (Z, K, X, Y)
ITERS = 2
TILE = 128
VECS = 256
OWN = 5
ROWS = OWN * TILE
GROUPS = 16
DESTS = 8
SLOTS = 120
HALF = 128
ROUTE = ROWS // 2
SUB = ROUTE // 2
BLOCK = 64
HIGHEST = lax.Precision.HIGHEST
MESH = pl.DeviceIdType.MESH
F32 = jnp.float32


def matmul(a, b, contract=((1,), (0,))):
    return lax.dot_general(
        a, b, (contract, ((), ())), precision=HIGHEST, preferred_element_type=F32
    )


def block_inverse(block):
    rows = lax.broadcasted_iota(jnp.int32, (BLOCK, 128), 0)
    lanes = lax.broadcasted_iota(jnp.int32, (BLOCK, 128), 1)
    e = jnp.where(lanes < BLOCK, block, jnp.where(lanes - BLOCK == rows, 1.0, 0.0))
    pivots = jnp.ones((BLOCK, 128), F32)
    for panel in range(BLOCK // 8):
        cols = [
            jnp.broadcast_to(e[:, 8 * panel + j : 8 * panel + j + 1], (BLOCK, 128))
            for j in range(8)
        ]
        for j in range(8):
            k = 8 * panel + j
            d = cols[j][k : k + 1, :]
            pivots = jnp.where(rows == k, d, pivots)
            f = jnp.where(rows > k, cols[j] * (1.0 / d), 0.0)
            for i in range(j + 1, 8):
                cols[i] = cols[i] - f * cols[i][k : k + 1, :]
            e = e - f * e[k : k + 1, :]
    return e * lax.rsqrt(pivots)


def inverse_factor(gram, aug, between=()):
    between = dict(between)
    aug[:, 0:VECS] = gram
    r = lax.broadcasted_iota(jnp.int32, (VECS, VECS), 0)
    c = lax.broadcasted_iota(jnp.int32, (VECS, VECS), 1)
    aug[:, VECS:] = jnp.where(r == c, 1.0, 0.0)
    for k0 in range(0, VECS, BLOCK):
        lo = k0 // 128 * 128
        hi = VECS + (k0 + BLOCK + 127) // 128 * 128
        block = aug[k0 : k0 + BLOCK, lo : lo + 128]
        if k0 > lo:
            block = pltpu.roll(block, 128 - (k0 - lo), 1)
        inverse = block_inverse(block)[:, BLOCK : 2 * BLOCK]
        panel = matmul(inverse, aug[k0 : k0 + BLOCK, lo:hi])
        aug[k0 : k0 + BLOCK, lo:hi] = panel
        if k0 + BLOCK < VECS:
            below = panel[:, : VECS - lo].T[k0 + BLOCK - lo :, :]
            aug[k0 + BLOCK :, lo:hi] = aug[k0 + BLOCK :, lo:hi] - matmul(below, panel)
        if k0 // BLOCK in between:
            between[k0 // BLOCK]()
    return aug[:, VECS:]


def place(axis, offset):
    return lax.rem(lax.axis_index(axis) + (offset + 4), 4)


class Sems:
    def __init__(self, send, recv):
        self.send, self.recv, self.used = send, recv, 0

    def copy(self, src, dst, device):
        i = self.used
        self.used += 1
        return pltpu.make_async_remote_copy(
            src_ref=src,
            dst_ref=dst,
            send_sem=self.send.at[i],
            recv_sem=self.recv.at[i],
            device_id=device,
            device_id_type=MESH,
        )


class Gather:
    def __init__(self, field, sems):
        self.field, self.sems, self.all = field, sems, []
        self.p1, self.q, self.f1, self.f2 = {}, {}, {}, {}

    def slot(self, route, d1, d2):
        dx, dy = (d1, d2) if route == 0 else (d2, d1)
        return place(X, dx) * 4 + place(Y, dy)

    def send(self, route, slot, start, size, along, sign):
        axis = (X, Y)[route ^ along]
        part = self.field.at[slot, pl.ds(route * ROUTE + start, size)]
        c = self.sems.copy(part, part, {axis: place(axis, sign)})
        c.start()
        self.all.append(c)
        return c

    def begin(self):
        for route in (0, 1):
            for s in (1, -1):
                self.p1[route, s] = self.send(route, self.slot(route, 0, 0), 0, ROUTE, 0, s)
        for route in (0, 1):
            self.spread(route, 0)

    def spread(self, route, d1):
        for s in (1, -1):
            self.q[route, d1, s] = self.send(route, self.slot(route, d1, 0), 0, ROUTE, 1, s)

    def sub(self, sign):
        return 0 if sign > 0 else SUB

    def near(self):
        for route in (0, 1):
            for s in (1, -1):
                self.p1[route, s].wait_recv()
                self.f1[route, s] = self.send(
                    route, self.slot(route, -s, 0), self.sub(s), SUB, 0, s
                )
        for route in (0, 1):
            for s in (1, -1):
                self.spread(route, -s)

    def far(self):
        for route in (0, 1):
            for s in (1, -1):
                self.f1[route, s].wait_recv()
            self.spread(route, 2)

    def onward(self, which):
        for d1 in which:
            for route in (0, 1):
                for s in (1, -1):
                    self.q[route, d1, s].wait_recv()
                    self.f2[route, d1, s] = self.send(
                        route, self.slot(route, d1, -s), self.sub(s), SUB, 1, s
                    )

    def finish(self):
        for c in self.f2.values():
            c.wait_recv()

    def sent(self):
        for c in self.all:
            c.wait_send()


class Scatter:
    def __init__(self, terms, pair, arrived, sems):
        self.terms, self.pair, self.arrived, self.sems = terms, pair, arrived, sems
        self.first, self.direct, self.last = {}, {}, {}

    def go(self, src, dst, device):
        c = self.sems.copy(src, dst, device)
        c.start()
        return c

    def begin(self):
        other = 1 - lax.axis_index(K)
        for d in (2, 1, -1, 0):
            self.first[d] = self.go(
                self.terms.at[other, place(Z, d)], self.pair.at[d % 4], {K: other}
            )

    def freed(self):
        for c in self.first.values():
            c.wait_send()

    def combine(self, d):
        self.first[d].wait_recv()
        mine = lax.axis_index(K)
        self.pair[d % 4] = self.pair[d % 4] + self.terms[mine, place(Z, d)]

    def rows(self, part):
        return pl.ds(part * ROUTE, ROUTE)

    def near(self):
        self.combine(2)
        for part, s in ((0, 1), (1, -1)):
            self.direct[2, s] = self.go(
                self.pair.at[2, self.rows(part)], self.arrived.at[part], {Z: place(Z, s)}
            )
        for part, s in ((1, 1), (0, -1)):
            self.combine(s)
            self.direct[1, s] = self.go(
                self.pair.at[s % 4, self.rows(part)], self.arrived.at[2 + part], {Z: place(Z, s)}
            )

    def onward(self):
        for part, s in ((0, 1), (1, -1)):
            self.direct[2, s].wait_recv()
            self.pair[s % 4, self.rows(part)] = (
                self.pair[s % 4, self.rows(part)] + self.arrived[part]
            )
            self.last[s] = self.go(
                self.pair.at[s % 4, self.rows(part)], self.arrived.at[4 + part], {Z: place(Z, s)}
            )
        self.combine(0)

    def total(self, put):
        for s in (1, -1):
            self.direct[1, s].wait_recv()
            self.last[s].wait_recv()
        for part in (0, 1):
            put(
                part,
                self.pair[0, self.rows(part)] + self.arrived[2 + part] + self.arrived[4 + part],
            )

    def sent(self):
        for c in (*self.direct.values(), *self.last.values()):
            c.wait_send()


def row_peers():
    for dx in range(4):
        for dy in range(4):
            if dx or dy:
                yield {X: place(X, dx), Y: place(Y, dy)}


def col_peers():
    for dk in range(2):
        for dz in range(4):
            if dk or dz:
                yield {Z: place(Z, dz), K: lax.rem(lax.axis_index(K) + dk, 2)}


def greet():
    barrier = pltpu.get_barrier_semaphore()
    count = 0
    for peer in (*row_peers(), *col_peers()):
        pl.semaphore_signal(barrier, inc=1, device_id=peer, device_id_type=MESH)
        count += 1
    pl.semaphore_wait(barrier, count)


class GramSum:
    def __init__(self, own, parts, piece, pieces, whole, sems):
        self.own, self.parts, self.piece, self.pieces, self.whole = own, parts, piece, pieces, whole
        self.sems, self.all = sems, []

    def go(self, src, dst, device):
        c = self.sems.copy(src, dst, device)
        c.start()
        self.all.append(c)
        return c

    def begin(self):
        me = lax.axis_index(X) * 4 + lax.axis_index(Y)
        self.one = [
            self.go(self.own.at[to[X] * 4 + to[Y]], self.parts.at[me], to) for to in row_peers()
        ]
        self.parts[me] = self.own[me]

    def across(self):
        for c in self.one:
            c.wait_recv()
        total = self.parts[0]
        for i in range(1, GROUPS):
            total = total + self.parts[i]
        self.piece[...] = total
        z, k = lax.axis_index(Z), lax.axis_index(K)
        me = z * 2 + k
        self.two = [self.go(self.piece, self.pieces.at[me], to) for to in col_peers()]
        self.pieces[me] = total

    def back(self):
        for c in self.two:
            c.wait_recv()
        total = self.pieces[0]
        for i in range(1, DESTS):
            total = total + self.pieces[i]
        me = lax.axis_index(X) * 4 + lax.axis_index(Y)
        self.whole[me] = total
        self.three = [self.go(self.whole.at[me], self.whole.at[me], to) for to in row_peers()]

    def result(self):
        for c in self.three:
            c.wait_recv()
        return self.whole[...].reshape(VECS, VECS)

    def sent(self):
        for c in self.all:
            c.wait_send()


GRAM_COPIES = 15 + 7 + 15
GATHER_COPIES = 40
SCATTER_COPIES = 10


def gram_scratch():
    return [
        pltpu.VMEM((GROUPS, 16, VECS), F32),
        pltpu.VMEM((GROUPS, 16, VECS), F32),
        pltpu.VMEM((16, VECS), F32),
        pltpu.VMEM((DESTS, 16, VECS), F32),
        pltpu.VMEM((GROUPS, 16, VECS), F32),
        pltpu.SemaphoreType.DMA((GRAM_COPIES,)),
        pltpu.SemaphoreType.DMA((GRAM_COPIES,)),
    ]


def gram_of(refs):
    return GramSum(*refs[:5], Sems(*refs[5:]))


def split_panels(field, split, scale):
    def group(r, _):
        if scale is not None:
            cols = scale[r]
        for t in range(OWN):
            v = field[r, pl.ds(t * TILE, TILE), :]
            if scale is not None:
                v = v * cols[:, t : t + 1]
            high = v.astype(jnp.bfloat16)
            split[r * OWN + t, 0:TILE, :] = high
            split[r * OWN + t, TILE:, :] = (v - high.astype(F32)).astype(jnp.bfloat16)
        return 0

    lax.fori_loop(0, GROUPS, group, 0)


UNROLL = 12


def tile_products(tiles, split, order, source, keep, running, between):
    def step(i, total):
        for j in range(UNROLL):
            s = i * UNROLL + j
            tile = tiles[order[s]]
            both = jnp.concatenate([tile, tile], axis=1)
            y = jnp.dot(both, split[source[s]], preferred_element_type=F32)
            total = y + keep[s] * total
            running[s] = total
        return total

    total = jnp.zeros((TILE, HALF), F32)
    steps = SLOTS // UNROLL
    parts = len(between) + 1
    for p in range(parts):
        total = lax.fori_loop(steps * p // parts, steps * (p + 1) // parts, step, total)
        if p < parts - 1:
            between[p]()


def tile_terms(running, last, has, terms):
    def dest(c, _):
        z, k = c // 2, lax.rem(c, 2)
        for t in range(OWN):
            i = c * OWN + t
            terms[k, z, pl.ds(t * TILE, TILE), :] = has[i] * running[last[i]]
        return 0

    lax.fori_loop(0, DESTS, dest, 0)


def load_tiles(affinity, tiles, sem):
    c = pltpu.make_async_copy(affinity, tiles, sem)
    c.start()
    return c


def spread_scale(row, scale):
    cols = row[...].T
    for t in range(OWN):
        scale[pl.ds(t * TILE, TILE), :] = jnp.broadcast_to(cols[:, t : t + 1], (TILE, 128))


def half(h):
    return pl.ds(h * HALF, HALF)


def sweeps_kernel(
    order, source, keep, last, has, start, affinity, vectors, firsts,
    tiles, field, split, running, terms, pair, arrived,
    image, scale, sums, degree_out, degree_in, scales, columns, aug, work,
    tile_sem, out_sem, gather_send, gather_recv, scatter_send, scatter_recv, small_send, small_recv, *gram_refs,
):
    tile_copy = load_tiles(affinity, tiles, tile_sem)
    x, y, z, k = (lax.axis_index(a) for a in (X, Y, Z, K))
    me, col = x * 4 + y, z * 2 + k
    g = [Gather(field.at[i], Sems(gather_send.at[i], gather_recv.at[i])) for i in range(4)]
    s = [
        Scatter(terms, pair.at[i], arrived.at[i], Sems(scatter_send.at[i], scatter_recv.at[i]))
        for i in range(4)
    ]
    grams = [gram_of(gram_refs[7 * i : 7 * i + 7]) for i in range(4)]
    root = jnp.sqrt(F32(ROWS * GROUPS * DESTS))
    small = Sems(small_send, small_recv)
    smalls = []
    for h in range(2):
        field[h, me] = start[:, h * HALF : (h + 1) * HALF]
    greet()
    g[0].begin()
    tile_copy.wait()

    ones = jnp.ones((8, TILE), jnp.bfloat16)

    def row_sums(i, total):
        for j in range(UNROLL):
            n = i * UNROLL + j
            d = lax.dot_general(
                ones, tiles[order[n]], (((1,), (1,)), ((), ())), preferred_element_type=F32
            )
            total = d + keep[n] * total
            sums[n] = total
        return total

    steps = SLOTS // UNROLL
    total = lax.fori_loop(0, steps // 3, row_sums, jnp.zeros((8, TILE), F32))
    g[0].near()
    total = lax.fori_loop(steps // 3, steps * 2 // 3, row_sums, total)
    g[0].far()
    g[1].begin()
    lax.fori_loop(steps * 2 // 3, steps, row_sums, total)
    for c in range(DESTS):
        for t in range(8):
            i = c * OWN + t
            if t < OWN:
                degree_out[c, t : t + 1, :] = (has[i] * sums[last[i]])[0:1]
            else:
                degree_out[c, t : t + 1, :] = jnp.zeros((1, TILE), F32)
    for to in col_peers():
        c = small.copy(degree_out.at[to[Z] * 2 + to[K]], degree_in.at[col], to)
        c.start()
        smalls.append(c)
    degree_in[col] = degree_out[col]
    g[0].onward((0,))
    for c in smalls:
        c.wait_recv()
    degree = degree_in[0]
    for c in range(1, DESTS):
        degree = degree + degree_in[c]
    scales[me] = 1.0 / jnp.sqrt(1.0 + degree)
    gathered = []
    for to in row_peers():
        c = small.copy(scales.at[me], scales.at[me], to)
        c.start()
        gathered.append(c)
    spread_scale(scales.at[me], scale)
    g[0].onward((1, -1))
    for c in gathered:
        c.wait_recv()

    def turn(r, _):
        columns[r, :, 0:8] = scales[r].T
        return 0

    lax.fori_loop(0, GROUPS, turn, 0)
    g[0].onward((2,))
    g[1].near()
    g[0].finish()

    def products(i, between):
        split_panels(field.at[i], split, columns if i < 2 else None)
        between[0]()
        tile_products(tiles, split, order, source, keep, running, between[1:])
        if i:
            s[i - 1].freed()
        tile_terms(running, last, has, terms)
        s[i].begin()

    def put(h, part, total):
        rows = pl.ds(part * ROUTE, ROUTE)
        r = scale[rows]
        v = r * (r * start[rows, half(h)] + total)
        image[rows, half(h)] = v
        field[2 + h, me, rows] = r * v

    def put_second(h, part, total):
        rows = pl.ds(part * ROUTE, ROUTE)
        vectors[rows, half(h)] = scale[rows] * (field[2 + h, me, rows] + total)

    def nothing():
        pass

    products(0, [nothing, g[1].far])
    g[1].onward((0,))
    s[0].near()
    g[1].onward((1, -1))
    s[0].onward()
    g[1].onward((2,))
    s[0].total(functools.partial(put, 0))
    g[2].begin()
    g[1].finish()
    products(1, [nothing, g[2].near])
    g[2].far()
    g[2].onward((0,))
    s[1].near()
    g[2].onward((1, -1))
    s[1].onward()
    g[2].onward((2,))
    s[1].total(functools.partial(put, 1))

    def local_gram(n, matrix):
        grams[n].own[...] = matmul(matrix, matrix, ((0,), (0,))).reshape(GROUPS, 16, VECS)
        grams[n].begin()

    local_gram(0, image[...])
    g[3].begin()
    grams[0].across()
    g[2].finish()
    products(2, [grams[0].back, g[3].near])
    inverse_one = inverse_factor(
        grams[0].result(),
        aug,
        {
            0: g[3].far,
            1: lambda: g[3].onward((0,)),
            2: lambda: (s[2].near(), g[3].onward((1, -1))),
            3: lambda: (s[2].onward(), g[3].onward((2,))),
        },
    )
    work[0] = inverse_one
    first = matmul(image[...], inverse_one, ((1,), (1,)))
    local_gram(1, first)
    image[...] = root * first
    first_out = [pltpu.make_async_copy(image, firsts.at[0], out_sem)]
    first_out[0].start()
    s[2].total(functools.partial(put_second, 0))
    grams[1].across()
    g[3].finish()
    products(3, [grams[1].back, nothing])
    inverse_two = inverse_factor(grams[1].result(), aug, {1: s[3].near, 3: s[3].onward})
    both = matmul(inverse_two, work[0])
    s[3].total(functools.partial(put_second, 1))
    mapped = matmul(vectors[...], both, ((1,), (1,)))
    local_gram(2, mapped)
    grams[2].across()
    grams[2].back()
    first = matmul(mapped, inverse_factor(grams[2].result(), aug), ((1,), (1,)))
    local_gram(3, first)
    first_out[0].wait()
    image[...] = root * first
    first_out.append(pltpu.make_async_copy(image, firsts.at[1], out_sem))
    first_out[1].start()
    grams[3].across()
    grams[3].back()
    vectors[...] = root * matmul(first, inverse_factor(grams[3].result(), aug), ((1,), (1,)))
    first_out[1].wait()
    s[3].freed()
    for c in smalls + gathered:
        c.wait_send()
    for c in (*g, *s, *grams):
        c.sent()


def slot_order(tile_rows, tile_cols, live_tiles):
    slot = jnp.arange(SLOTS)
    key = jnp.where(slot < live_tiles[0], tile_rows, DESTS * OWN)
    before = (key[None, :] < key[:, None]) | (
        (key[None, :] == key[:, None]) & (slot[None, :] < slot[:, None])
    )
    rank = jnp.sum(before.astype(jnp.int32), axis=1)
    at = rank[None, :] == slot[:, None]
    order = jnp.sum(jnp.where(at, slot[None, :], 0), axis=1)
    source = jnp.sum(jnp.where(at, tile_cols[None, :], 0), axis=1)
    follows = (rank[None, :] == slot[:, None] - 1).astype(jnp.int32)
    keys = jnp.sum(jnp.where(at, key[None, :], 0), axis=1)
    previous = jnp.sum(follows * (key[None, :] + 1), axis=1) - 1
    keep = (keys == previous).astype(F32)
    row = jnp.arange(DESTS * OWN)
    last = jnp.maximum(jnp.sum((key[None, :] <= row[:, None]).astype(jnp.int32), axis=1) - 1, 0)
    has = jnp.any(key[None, :] == row[:, None], axis=1).astype(F32)
    return order.astype(jnp.int32), source.astype(jnp.int32), keep, last, has


def body(affinity, tile_rows, tile_cols, live_tiles, start):
    slots = slot_order(tile_rows, tile_cols, live_tiles)
    smem = pl.BlockSpec(memory_space=pltpu.SMEM)
    vmem = pl.BlockSpec(memory_space=pltpu.VMEM)
    anywhere = pl.BlockSpec(memory_space=pl.ANY)
    dma = pltpu.SemaphoreType.DMA
    return pl.pallas_call(
        sweeps_kernel,
        out_shape=(
            jax.ShapeDtypeStruct((ROWS, VECS), F32),
            jax.ShapeDtypeStruct((ITERS, ROWS, VECS), F32),
        ),
        in_specs=[smem] * 5 + [vmem, anywhere],
        out_specs=(vmem, anywhere),
        scratch_shapes=[
            pltpu.VMEM((SLOTS, TILE, TILE), jnp.bfloat16),
            pltpu.VMEM((4, GROUPS, ROWS, HALF), F32),
            pltpu.VMEM((GROUPS * OWN, 2 * TILE, HALF), jnp.bfloat16),
            pltpu.VMEM((SLOTS, TILE, HALF), F32),
            pltpu.VMEM((2, 4, ROWS, HALF), F32),
            pltpu.VMEM((4, 4, ROWS, HALF), F32),
            pltpu.VMEM((4, 6, ROUTE, HALF), F32),
            pltpu.VMEM((ROWS, VECS), F32),
            pltpu.VMEM((ROWS, HALF), F32),
            pltpu.VMEM((SLOTS, 8, TILE), F32),
            pltpu.VMEM((DESTS, 8, TILE), F32),
            pltpu.VMEM((DESTS, 8, TILE), F32),
            pltpu.VMEM((GROUPS, 8, TILE), F32),
            pltpu.VMEM((GROUPS, TILE, TILE), F32),
            pltpu.VMEM((VECS, 2 * VECS), F32),
            pltpu.VMEM((1, VECS, VECS), F32),
            dma,
            dma,
            dma((4, GATHER_COPIES)),
            dma((4, GATHER_COPIES)),
            dma((4, SCATTER_COPIES)),
            dma((4, SCATTER_COPIES)),
            dma((22,)),
            dma((22,)),
        ]
        + gram_scratch() * 4,
        compiler_params=pltpu.CompilerParams(
            collective_id=0, has_side_effects=True, vmem_limit_bytes=60 << 20
        ),
        name="sweeps",
    )(*slots, start, affinity)


def solution(mesh):
    torus = Mesh(mesh.devices.reshape(4, 2, 4, 4), COL_ROW)
    return jax.shard_map(
        body,
        mesh=torus,
        in_specs=(P(COL_ROW, None, None), P(COL_ROW), P(COL_ROW), P(COL_ROW), P(COL_ROW, None)),
        out_specs=(P(COL_ROW, None), P(None, COL_ROW, None)),
        check_vma=False,
    )
```

```python
import functools

import jax
import jax.numpy as jnp
from jax import lax
from jax.experimental import pallas as pl
from jax.experimental.pallas import tpu as pltpu
from jax.sharding import Mesh
from jax.sharding import PartitionSpec as P

Z, K, X, Y = "z", "k", "x", "y"
COL_ROW = (Z, K, X, Y)
ITERS = 2
TILE = 128
VECS = 256
OWN = 5
ROWS = OWN * TILE
GROUPS = 16
DESTS = 8
SLOTS = 120
HALF = 128
ROUTE = ROWS // 2
SUB = ROUTE // 2
BLOCK = 64
HIGHEST = lax.Precision.HIGHEST
MESH = pl.DeviceIdType.MESH
F32 = jnp.float32


def matmul(a, b, contract=((1,), (0,))):
    return lax.dot_general(
        a, b, (contract, ((), ())), precision=HIGHEST, preferred_element_type=F32
    )


def thirds(a):
    high = a.astype(jnp.bfloat16)
    rest = a - high.astype(F32)
    middle = rest.astype(jnp.bfloat16)
    return high, middle, (rest - middle.astype(F32)).astype(jnp.bfloat16)


def short_matmul(a, b):
    ah, am, al = thirds(a)
    bh, bm, bl = thirds(b)
    return jnp.dot(
        jnp.concatenate([ah, ah, am, ah, am, al], axis=1),
        jnp.concatenate([bh, bm, bh, bl, bm, bh], axis=0),
        preferred_element_type=F32,
    )


def close_matmul(a, b, contract):
    axis_a, axis_b = contract[0][0], contract[1][0]
    ah, bh = a.astype(jnp.bfloat16), b.astype(jnp.bfloat16)
    al = (a - ah.astype(F32)).astype(jnp.bfloat16)
    bl = (b - bh.astype(F32)).astype(jnp.bfloat16)
    return lax.dot_general(
        jnp.concatenate([ah, ah, al], axis=axis_a),
        jnp.concatenate([bh, bl, bh], axis=axis_b),
        (contract, ((), ())),
        preferred_element_type=F32,
    )


def block_inverse(block):
    rows = lax.broadcasted_iota(jnp.int32, (BLOCK, 128), 0)
    lanes = lax.broadcasted_iota(jnp.int32, (BLOCK, 128), 1)
    e = jnp.where(lanes < BLOCK, block, jnp.where(lanes - BLOCK == rows, 1.0, 0.0))
    pivots = jnp.ones((BLOCK, 128), F32)
    for panel in range(BLOCK // 8):
        cols = [
            jnp.broadcast_to(e[:, 8 * panel + j : 8 * panel + j + 1], (BLOCK, 128))
            for j in range(8)
        ]
        for j in range(8):
            k = 8 * panel + j
            d = cols[j][k : k + 1, :]
            pivots = jnp.where(rows == k, d, pivots)
            f = jnp.where(rows > k, cols[j] * (1.0 / d), 0.0)
            for i in range(j + 1, 8):
                cols[i] = cols[i] - f * cols[i][k : k + 1, :]
            e = e - f * e[k : k + 1, :]
    return e * lax.rsqrt(pivots)


def inverse_factor(gram, aug, between=()):
    between = dict(between)
    aug[:, 0:VECS] = gram
    r = lax.broadcasted_iota(jnp.int32, (VECS, VECS), 0)
    c = lax.broadcasted_iota(jnp.int32, (VECS, VECS), 1)
    aug[:, VECS:] = jnp.where(r == c, 1.0, 0.0)
    for k0 in range(0, VECS, BLOCK):
        lo = k0 // 128 * 128
        hi = VECS + (k0 + BLOCK + 127) // 128 * 128
        block = aug[k0 : k0 + BLOCK, lo : lo + 128]
        if k0 > lo:
            block = pltpu.roll(block, 128 - (k0 - lo), 1)
        inverse = block_inverse(block)[:, BLOCK : 2 * BLOCK]
        panel = short_matmul(inverse, aug[k0 : k0 + BLOCK, lo:hi])
        aug[k0 : k0 + BLOCK, lo:hi] = panel
        if k0 + BLOCK < VECS:
            below = panel[:, : VECS - lo].T[k0 + BLOCK - lo :, :]
            aug[k0 + BLOCK :, lo:hi] = aug[k0 + BLOCK :, lo:hi] - short_matmul(below, panel)
        if k0 // BLOCK in between:
            between[k0 // BLOCK]()
    return aug[:, VECS:]


def place(axis, offset):
    return lax.rem(lax.axis_index(axis) + (offset + 4), 4)


class Sems:
    def __init__(self, send, recv):
        self.send, self.recv, self.used = send, recv, 0

    def copy(self, src, dst, device):
        i = self.used
        self.used += 1
        return pltpu.make_async_remote_copy(
            src_ref=src,
            dst_ref=dst,
            send_sem=self.send.at[i],
            recv_sem=self.recv.at[i],
            device_id=device,
            device_id_type=MESH,
        )


class Gather:
    def __init__(self, field, sems):
        self.field, self.sems, self.all = field, sems, []
        self.p1, self.q, self.f1, self.f2 = {}, {}, {}, {}

    def slot(self, route, d1, d2):
        dx, dy = (d1, d2) if route == 0 else (d2, d1)
        return place(X, dx) * 4 + place(Y, dy)

    def send(self, route, slot, start, size, along, sign):
        axis = (X, Y)[route ^ along]
        part = self.field.at[slot, pl.ds(route * ROUTE + start, size)]
        c = self.sems.copy(part, part, {axis: place(axis, sign)})
        c.start()
        self.all.append(c)
        return c

    def begin(self):
        for route in (0, 1):
            for s in (1, -1):
                self.p1[route, s] = self.send(route, self.slot(route, 0, 0), 0, ROUTE, 0, s)

    def own(self):
        for route in (0, 1):
            self.spread(route, 0)

    def spread(self, route, d1):
        for s in (1, -1):
            self.q[route, d1, s] = self.send(route, self.slot(route, d1, 0), 0, ROUTE, 1, s)

    def sub(self, sign):
        return 0 if sign > 0 else SUB

    def near(self):
        for route in (0, 1):
            for s in (1, -1):
                self.p1[route, s].wait_recv()
                self.f1[route, s] = self.send(
                    route, self.slot(route, -s, 0), self.sub(s), SUB, 0, s
                )
        for route in (0, 1):
            for s in (1, -1):
                self.spread(route, -s)

    def far(self):
        for route in (0, 1):
            for s in (1, -1):
                self.f1[route, s].wait_recv()
            self.spread(route, 2)

    def onward(self, which):
        for d1 in which:
            for route in (0, 1):
                for s in (1, -1):
                    self.q[route, d1, s].wait_recv()
                    self.f2[route, d1, s] = self.send(
                        route, self.slot(route, d1, -s), self.sub(s), SUB, 1, s
                    )

    def finish(self):
        for c in self.f2.values():
            c.wait_recv()

    def sent(self):
        for c in self.all:
            c.wait_send()


class Scatter:
    def __init__(self, terms, pair, arrived, sems):
        self.terms, self.pair, self.arrived, self.sems = terms, pair, arrived, sems
        self.first, self.direct, self.last = {}, {}, {}

    def go(self, src, dst, device):
        c = self.sems.copy(src, dst, device)
        c.start()
        return c

    def begin(self):
        other = 1 - lax.axis_index(K)
        for d in (2, 1, -1, 0):
            self.first[d] = self.go(
                self.terms.at[other, place(Z, d)], self.pair.at[d % 4], {K: other}
            )

    def freed(self):
        for c in self.first.values():
            c.wait_send()

    def combine(self, d):
        self.first[d].wait_recv()
        mine = lax.axis_index(K)
        self.pair[d % 4] = self.pair[d % 4] + self.terms[mine, place(Z, d)]

    def rows(self, part):
        return pl.ds(part * ROUTE, ROUTE)

    def near(self):
        self.combine(2)
        for part, s in ((0, 1), (1, -1)):
            self.direct[2, s] = self.go(
                self.pair.at[2, self.rows(part)], self.arrived.at[part], {Z: place(Z, s)}
            )
        for part, s in ((1, 1), (0, -1)):
            self.combine(s)
            self.direct[1, s] = self.go(
                self.pair.at[s % 4, self.rows(part)], self.arrived.at[2 + part], {Z: place(Z, s)}
            )

    def onward(self):
        for part, s in ((0, 1), (1, -1)):
            self.direct[2, s].wait_recv()
            self.pair[s % 4, self.rows(part)] = (
                self.pair[s % 4, self.rows(part)] + self.arrived[part]
            )
            self.last[s] = self.go(
                self.pair.at[s % 4, self.rows(part)], self.arrived.at[4 + part], {Z: place(Z, s)}
            )
        self.combine(0)

    def total(self, put):
        for s in (1, -1):
            self.direct[1, s].wait_recv()
            self.last[s].wait_recv()
        for part in (0, 1):
            put(
                part,
                self.pair[0, self.rows(part)] + self.arrived[2 + part] + self.arrived[4 + part],
            )

    def sent(self):
        for c in (*self.direct.values(), *self.last.values()):
            c.wait_send()


def row_peers():
    for dx in range(4):
        for dy in range(4):
            if dx or dy:
                yield {X: place(X, dx), Y: place(Y, dy)}


def col_peers():
    for dk in range(2):
        for dz in range(4):
            if dk or dz:
                yield {Z: place(Z, dz), K: lax.rem(lax.axis_index(K) + dk, 2)}


def greet():
    barrier = pltpu.get_barrier_semaphore()
    count = 0
    for peer in (*row_peers(), *col_peers()):
        pl.semaphore_signal(barrier, inc=1, device_id=peer, device_id_type=MESH)
        count += 1
    pl.semaphore_wait(barrier, count)


class GramSum:
    def __init__(self, own, parts, piece, pieces, whole, sems):
        self.own, self.parts, self.piece, self.pieces, self.whole = own, parts, piece, pieces, whole
        self.sems, self.all = sems, []

    def go(self, src, dst, device):
        c = self.sems.copy(src, dst, device)
        c.start()
        self.all.append(c)
        return c

    def begin(self):
        me = lax.axis_index(X) * 4 + lax.axis_index(Y)
        self.one = [
            self.go(self.own.at[to[X] * 4 + to[Y]], self.parts.at[me], to) for to in row_peers()
        ]
        self.parts[me] = self.own[me]

    def across(self):
        for c in self.one:
            c.wait_recv()
        total = self.parts[0]
        for i in range(1, GROUPS):
            total = total + self.parts[i]
        self.piece[...] = total
        z, k = lax.axis_index(Z), lax.axis_index(K)
        me = z * 2 + k
        self.two = [self.go(self.piece, self.pieces.at[me], to) for to in col_peers()]
        self.pieces[me] = total

    def back(self):
        for c in self.two:
            c.wait_recv()
        total = self.pieces[0]
        for i in range(1, DESTS):
            total = total + self.pieces[i]
        me = lax.axis_index(X) * 4 + lax.axis_index(Y)
        self.whole[me] = total
        self.three = [self.go(self.whole.at[me], self.whole.at[me], to) for to in row_peers()]

    def result(self):
        for c in self.three:
            c.wait_recv()
        return self.whole[...].reshape(VECS, VECS)

    def sent(self):
        for c in self.all:
            c.wait_send()


GRAM_COPIES = 15 + 7 + 15
GATHER_COPIES = 40
SCATTER_COPIES = 10


def gram_scratch():
    return [
        pltpu.VMEM((GROUPS, 16, VECS), F32),
        pltpu.VMEM((GROUPS, 16, VECS), F32),
        pltpu.VMEM((16, VECS), F32),
        pltpu.VMEM((DESTS, 16, VECS), F32),
        pltpu.VMEM((GROUPS, 16, VECS), F32),
        pltpu.SemaphoreType.DMA((GRAM_COPIES,)),
        pltpu.SemaphoreType.DMA((GRAM_COPIES,)),
    ]


def gram_of(refs):
    return GramSum(*refs[:5], Sems(*refs[5:]))


def split_panels(field, split, scale):
    def group(r, _):
        if scale is not None:
            cols = scale[r]
        for t in range(OWN):
            v = field[r, pl.ds(t * TILE, TILE), :]
            if scale is not None:
                v = v * cols[:, t : t + 1]
            high = v.astype(jnp.bfloat16)
            split[r * OWN + t, 0:TILE, :] = high
            split[r * OWN + t, TILE:, :] = (v - high.astype(F32)).astype(jnp.bfloat16)
        return 0

    lax.fori_loop(0, GROUPS, group, 0)


UNROLL = 24


def tile_products(tiles, split, order, source, keep, running, between):
    def step(i, total):
        for j in range(UNROLL):
            s = i * UNROLL + j
            tile = tiles[order[s]]
            both = jnp.concatenate([tile, tile], axis=1)
            y = jnp.dot(both, split[source[s]], preferred_element_type=F32)
            total = y + keep[s] * total
            running[s] = total
        return total

    total = jnp.zeros((TILE, HALF), F32)
    steps = SLOTS // UNROLL
    parts = len(between) + 1
    for p in range(parts):
        total = lax.fori_loop(steps * p // parts, steps * (p + 1) // parts, step, total)
        if p < parts - 1:
            between[p]()


def tile_terms(running, last, has, terms):
    def dest(c, _):
        z, k = c // 2, lax.rem(c, 2)
        for t in range(OWN):
            i = c * OWN + t
            terms[k, z, pl.ds(t * TILE, TILE), :] = has[i] * running[last[i]]
        return 0

    lax.fori_loop(0, DESTS, dest, 0)


def load_tiles(affinity, tiles, sem):
    c = pltpu.make_async_copy(affinity, tiles, sem)
    c.start()
    return c


def spread_scale(row, scale):
    cols = row[...].T
    for t in range(OWN):
        scale[pl.ds(t * TILE, TILE), :] = jnp.broadcast_to(cols[:, t : t + 1], (TILE, 128))


def half(h):
    return pl.ds(h * HALF, HALF)


def sweeps_kernel(
    order, source, keep, last, has, start, affinity, vectors, firsts,
    tiles, field, split, running, terms, pair, arrived,
    image, scale, sums, degree_out, degree_in, scales, columns, aug, work,
    tile_sem, out_sem, gather_send, gather_recv, scatter_send, scatter_recv, small_send, small_recv, *gram_refs,
):
    tile_copy = load_tiles(affinity, tiles, tile_sem)
    x, y, z, k = (lax.axis_index(a) for a in (X, Y, Z, K))
    me, col = x * 4 + y, z * 2 + k
    g = [Gather(field.at[i], Sems(gather_send.at[i], gather_recv.at[i])) for i in range(4)]
    s = [
        Scatter(terms, pair.at[i], arrived.at[i], Sems(scatter_send.at[i], scatter_recv.at[i]))
        for i in range(4)
    ]
    grams = [gram_of(gram_refs[7 * i : 7 * i + 7]) for i in range(4)]
    root = jnp.sqrt(F32(ROWS * GROUPS * DESTS))
    small = Sems(small_send, small_recv)
    smalls = []
    for h in range(2):
        field[h, me] = start[:, h * HALF : (h + 1) * HALF]
    greet()
    g[0].begin()
    g[0].own()
    tile_copy.wait()

    ones = jnp.ones((8, TILE), jnp.bfloat16)

    def row_sums(i, total):
        for j in range(UNROLL):
            n = i * UNROLL + j
            d = lax.dot_general(
                ones, tiles[order[n]], (((1,), (1,)), ((), ())), preferred_element_type=F32
            )
            total = d + keep[n] * total
            sums[n] = total
        return total

    steps = SLOTS // UNROLL
    total = lax.fori_loop(0, steps // 3, row_sums, jnp.zeros((8, TILE), F32))
    g[0].near()
    total = lax.fori_loop(steps // 3, steps * 2 // 3, row_sums, total)
    g[0].far()
    g[1].begin()
    g[1].own()
    lax.fori_loop(steps * 2 // 3, steps, row_sums, total)
    for c in range(DESTS):
        for t in range(8):
            i = c * OWN + t
            if t < OWN:
                degree_out[c, t : t + 1, :] = (has[i] * sums[last[i]])[0:1]
            else:
                degree_out[c, t : t + 1, :] = jnp.zeros((1, TILE), F32)
    for to in col_peers():
        c = small.copy(degree_out.at[to[Z] * 2 + to[K]], degree_in.at[col], to)
        c.start()
        smalls.append(c)
    degree_in[col] = degree_out[col]
    g[0].onward((0,))
    for c in smalls:
        c.wait_recv()
    degree = degree_in[0]
    for c in range(1, DESTS):
        degree = degree + degree_in[c]
    scales[me] = 1.0 / jnp.sqrt(1.0 + degree)
    gathered = []
    for to in row_peers():
        c = small.copy(scales.at[me], scales.at[me], to)
        c.start()
        gathered.append(c)
    spread_scale(scales.at[me], scale)
    g[0].onward((1, -1))
    for c in gathered:
        c.wait_recv()

    def turn(r, _):
        columns[r, :, 0:8] = scales[r].T
        return 0

    lax.fori_loop(0, GROUPS, turn, 0)
    g[0].onward((2,))
    g[1].near()
    g[0].finish()

    def products(i, between):
        split_panels(field.at[i], split, columns if i < 2 else None)
        between[0]()
        tile_products(tiles, split, order, source, keep, running, between[1:])
        if i:
            s[i - 1].freed()
        tile_terms(running, last, has, terms)
        s[i].begin()

    def put(h, part, total):
        rows = pl.ds(part * ROUTE, ROUTE)
        r = scale[rows]
        v = r * (r * start[rows, half(h)] + total)
        image[rows, half(h)] = v
        field[2 + h, me, rows] = r * v

    def put_second(h, part, total):
        rows = pl.ds(part * ROUTE, ROUTE)
        vectors[rows, half(h)] = scale[rows] * (field[2 + h, me, rows] + total)

    def nothing():
        pass

    products(0, [nothing, g[1].far])
    g[1].onward((0,))
    s[0].near()
    g[1].onward((1, -1))
    s[0].onward()
    g[1].onward((2,))
    s[0].total(functools.partial(put, 0))
    g[2].begin()
    g[2].own()
    g[1].finish()
    products(1, [nothing, g[2].near])
    g[2].far()
    g[2].onward((0,))
    s[1].near()
    g[2].onward((1, -1))
    s[1].onward()
    g[2].onward((2,))
    s[1].total(functools.partial(put, 1))

    def local_gram(n, matrix, product=matmul):
        grams[n].own[...] = product(matrix, matrix, ((0,), (0,))).reshape(GROUPS, 16, VECS)
        grams[n].begin()

    local_gram(0, image[...])
    g[3].begin()
    g[3].own()
    grams[0].across()
    g[2].finish()
    products(2, [grams[0].back, g[3].near])
    inverse_one = inverse_factor(
        grams[0].result(),
        aug,
        {
            0: g[3].far,
            1: lambda: g[3].onward((0,)),
            2: lambda: (s[2].near(), g[3].onward((1, -1))),
            3: lambda: (s[2].onward(), g[3].onward((2,))),
        },
    )
    work[0] = inverse_one
    first = matmul(image[...], inverse_one, ((1,), (1,)))
    local_gram(1, first, close_matmul)
    image[...] = root * first
    first_out = [pltpu.make_async_copy(image, firsts.at[0], out_sem)]
    first_out[0].start()
    s[2].total(functools.partial(put_second, 0))
    grams[1].across()
    g[3].finish()
    products(3, [grams[1].back, nothing])
    inverse_two = inverse_factor(grams[1].result(), aug, {1: s[3].near, 3: s[3].onward})
    both = matmul(inverse_two, work[0])
    s[3].total(functools.partial(put_second, 1))
    mapped = matmul(vectors[...], both, ((1,), (1,)))
    local_gram(2, mapped)
    grams[2].across()
    grams[2].back()
    first = matmul(mapped, inverse_factor(grams[2].result(), aug), ((1,), (1,)))
    local_gram(3, first, close_matmul)
    first_out[0].wait()
    image[...] = root * first
    first_out.append(pltpu.make_async_copy(image, firsts.at[1], out_sem))
    first_out[1].start()
    grams[3].across()
    grams[3].back()
    vectors[...] = root * close_matmul(first, inverse_factor(grams[3].result(), aug), ((1,), (1,)))
    first_out[1].wait()
    s[3].freed()
    for c in smalls + gathered:
        c.wait_send()
    for c in (*g, *s, *grams):
        c.sent()


def slot_order(tile_rows, tile_cols, live_tiles):
    slot = jnp.arange(SLOTS)
    key = jnp.where(slot < live_tiles[0], tile_rows, DESTS * OWN)
    before = (key[None, :] < key[:, None]) | (
        (key[None, :] == key[:, None]) & (slot[None, :] < slot[:, None])
    )
    rank = jnp.sum(before.astype(jnp.int32), axis=1)
    at = rank[None, :] == slot[:, None]
    order = jnp.sum(jnp.where(at, slot[None, :], 0), axis=1)
    source = jnp.sum(jnp.where(at, tile_cols[None, :], 0), axis=1)
    follows = (rank[None, :] == slot[:, None] - 1).astype(jnp.int32)
    keys = jnp.sum(jnp.where(at, key[None, :], 0), axis=1)
    previous = jnp.sum(follows * (key[None, :] + 1), axis=1) - 1
    keep = (keys == previous).astype(F32)
    row = jnp.arange(DESTS * OWN)
    last = jnp.maximum(jnp.sum((key[None, :] <= row[:, None]).astype(jnp.int32), axis=1) - 1, 0)
    has = jnp.any(key[None, :] == row[:, None], axis=1).astype(F32)
    return order.astype(jnp.int32), source.astype(jnp.int32), keep, last, has


def body(affinity, tile_rows, tile_cols, live_tiles, start):
    slots = slot_order(tile_rows, tile_cols, live_tiles)
    smem = pl.BlockSpec(memory_space=pltpu.SMEM)
    vmem = pl.BlockSpec(memory_space=pltpu.VMEM)
    anywhere = pl.BlockSpec(memory_space=pl.ANY)
    dma = pltpu.SemaphoreType.DMA
    return pl.pallas_call(
        sweeps_kernel,
        out_shape=(
            jax.ShapeDtypeStruct((ROWS, VECS), F32),
            jax.ShapeDtypeStruct((ITERS, ROWS, VECS), F32),
        ),
        in_specs=[smem] * 5 + [vmem, anywhere],
        out_specs=(vmem, anywhere),
        scratch_shapes=[
            pltpu.VMEM((SLOTS, TILE, TILE), jnp.bfloat16),
            pltpu.VMEM((4, GROUPS, ROWS, HALF), F32),
            pltpu.VMEM((GROUPS * OWN, 2 * TILE, HALF), jnp.bfloat16),
            pltpu.VMEM((SLOTS, TILE, HALF), F32),
            pltpu.VMEM((2, 4, ROWS, HALF), F32),
            pltpu.VMEM((4, 4, ROWS, HALF), F32),
            pltpu.VMEM((4, 6, ROUTE, HALF), F32),
            pltpu.VMEM((ROWS, VECS), F32),
            pltpu.VMEM((ROWS, HALF), F32),
            pltpu.VMEM((SLOTS, 8, TILE), F32),
            pltpu.VMEM((DESTS, 8, TILE), F32),
            pltpu.VMEM((DESTS, 8, TILE), F32),
            pltpu.VMEM((GROUPS, 8, TILE), F32),
            pltpu.VMEM((GROUPS, TILE, TILE), F32),
            pltpu.VMEM((VECS, 2 * VECS), F32),
            pltpu.VMEM((1, VECS, VECS), F32),
            dma,
            dma,
            dma((4, GATHER_COPIES)),
            dma((4, GATHER_COPIES)),
            dma((4, SCATTER_COPIES)),
            dma((4, SCATTER_COPIES)),
            dma((22,)),
            dma((22,)),
        ]
        + gram_scratch() * 4,
        compiler_params=pltpu.CompilerParams(
            collective_id=0, has_side_effects=True, vmem_limit_bytes=60 << 20
        ),
        name="sweeps",
    )(*slots, start, affinity)


def solution(mesh):
    torus = Mesh(mesh.devices.reshape(4, 2, 4, 4), COL_ROW)
    return jax.shard_map(
        body,
        mesh=torus,
        in_specs=(P(COL_ROW, None, None), P(COL_ROW), P(COL_ROW), P(COL_ROW), P(COL_ROW, None)),
        out_specs=(P(COL_ROW, None), P(None, COL_ROW, None)),
        check_vma=False,
    )
```
